32 devices in a mesh: groups: 2 (over x), row: 16 (over z, y, core).
Axes of the slice: x: 2, y: 2, z: 4, core: 2. Of those that a mesh axis runs over, the one named last changes fastest.
Arguments:
- embeddings: bfloat16 [16384, 4096], P(('groups', 'row')), parts along dimension 0, may hold values from -64 to 64
- basis: bfloat16 [4096, 256], replicated, may hold values from -0.09375 to 0.09375
- cluster_ids: int32 [16384], P(('groups', 'row')), parts along dimension 0, may hold values from 0 to 127, as said below
- member_order: int32 [16384], P(('groups', 'row')), parts along dimension 0, may hold values from 0 to 1935, as said below
- owner_map: int32 [256], P('groups'), parts along dimension 0, may hold values from 0 to 15, as said below
- counts: int32 [256], P(('groups', 'row')), parts along dimension 0, may hold values from 1 to 1936, as said below
Outputs:
- best: float32 [16384], P(('groups', 'row')), parts along dimension 0
- cluster_scores: float32 [256], P(('groups', 'row')), parts along dimension 0
The draws below stay inside these ranges and needn't reach their ends.
There are 2 independent parts, one for each index of `groups`. The reference program is written for one: setup_inputs(seed, part) draws one part's arguments, and reference() takes and returns one part's arrays. A program takes and returns all parts, laid end to end along the dimension named above; an argument that names none is the same for every part. Nothing has to cross between parts.
Inputs may be any that keep to these rules, and one draw needn't show every extreme that they name: `cluster_ids`: among the documents of one device's rows, at most 128 lie in clusters of one owner; in every draw some owner gets exactly 128 from every device. `member_order`: the members of each cluster carry the numbers 0 to its count - 1, each once. `owner_map`: each owner holds exactly 8 clusters. `counts`: the number of documents with this cluster id.
All inputs are finite; a program needn't handle non-finite values.
Results may differ from the reference program's by a relative error of at most 0.00061.
Values may be sent and summed in bfloat16 or wider, within the bound.
A program may use at most 64 MiB of HBM per device.

```python
import math
import jax
import jax.numpy as jnp
from jax import lax

E = 4096
P_SIZE = 256
DOC_DEV = 512
CL_DEV = 8
CAP = 128
N_ROW = 16


def routing_draw(key):
    key_perm, key_hot, key_tokens, key_ranks = jax.random.split(key, 4)
    cluster_total = CL_DEV * N_ROW
    doc_total = DOC_DEV * N_ROW
    shuffled = jax.random.permutation(key_perm, cluster_total).astype(jnp.int32)
    owner_map = jnp.zeros((cluster_total,), jnp.int32).at[shuffled].set(jnp.arange(cluster_total, dtype=jnp.int32) // CL_DEV)
    owned = shuffled.reshape(N_ROW, CL_DEV)
    hottest = jax.random.randint(key_hot, (), 0, N_ROW).astype(jnp.int32)
    remaining = DOC_DEV - CAP

    def one_source(source_key, source_index):
        key_pick, key_mix, key_local = jax.random.split(source_key, 3)
        tokens = jax.random.permutation(key_pick, (N_ROW - 1) * CAP)[:remaining].astype(jnp.int32)
        others = tokens // CAP
        others = others + (others >= hottest).astype(jnp.int32)
        owners = jnp.concatenate([jnp.full((CAP,), hottest, jnp.int32), others])
        owners = jax.random.permutation(key_mix, owners)
        local = jax.random.randint(key_local, (DOC_DEV,), 0, CL_DEV).astype(jnp.int32)
        is_hot = owners == hottest
        hot_rank = jnp.cumsum(is_hot.astype(jnp.int32)) - 1
        hot_local = jnp.where(source_index == 0, hot_rank % CL_DEV, 0).astype(jnp.int32)
        local = jnp.where(is_hot, hot_local, local)
        return (owners, local)
    owners, local = jax.vmap(one_source)(jax.random.split(key_tokens, N_ROW), jnp.arange(N_ROW, dtype=jnp.int32))
    cluster_ids = owned[owners, local].reshape(-1).astype(jnp.int32)
    counts = jax.ops.segment_sum(jnp.ones((doc_total,), jnp.int32), cluster_ids, num_segments=cluster_total)
    shuffle_rank = jax.random.permutation(key_ranks, doc_total).astype(jnp.int32)
    ordering = jnp.argsort(cluster_ids * doc_total + shuffle_rank)
    starts = jnp.cumsum(counts) - counts
    position = jnp.arange(doc_total, dtype=jnp.int32) - starts[cluster_ids[ordering]]
    member_order = jnp.zeros((doc_total,), jnp.int32).at[ordering].set(position)
    return (cluster_ids, member_order, owner_map, counts.astype(jnp.int32))


def draw_cluster_ids(key, part):
    drawn = routing_draw(key)
    return drawn[0]


def draw_member_order(key, part):
    drawn = routing_draw(key)
    return drawn[1]


def draw_owner_map(key, part):
    drawn = routing_draw(key)
    return drawn[2]


def draw_counts(key, part):
    drawn = routing_draw(key)
    return drawn[3]


def draw_embeddings(key, part):
    cluster_ids = routing_draw(key)[0]
    key = jax.random.fold_in(key, 11)
    key_center, key_noise, key_mix, key_strength = jax.random.split(key, 4)
    doc_total = DOC_DEV * N_ROW
    centers = jax.random.normal(key_center, (CL_DEV * N_ROW, E), jnp.float32)
    strength = jnp.exp(jax.random.uniform(key_strength, (CL_DEV * N_ROW, 1), jnp.float32, math.log(0.3), math.log(2.0)))
    mix = jax.random.uniform(key_mix, (doc_total, 1), jnp.float32, 0.5, 1.5) * strength[cluster_ids]
    noise = jax.random.normal(key_noise, (doc_total, E), jnp.float32)
    values = mix * centers[cluster_ids] + noise
    return jnp.clip(values, -64.0, 64.0).astype(jnp.bfloat16)


def centred(stream_key, dims, scale, most, held_as=jnp.bfloat16):
    return jnp.clip(scale * jax.random.normal(stream_key, dims, jnp.float32), -most, most).astype(held_as)


def setup_inputs(seed: int = 0, part: int = 0) -> dict:
    key_list = jax.random.split(jax.random.key(seed), 7)
    own_keys = jax.random.split(jax.random.fold_in(key_list[6], part), 7)
    embeddings = draw_embeddings(jax.random.fold_in(jax.random.fold_in(key_list[6], part), 71), part)
    basis = centred(key_list[1], (E, P_SIZE), E ** -0.5, 0.09375)
    cluster_ids = draw_cluster_ids(jax.random.fold_in(jax.random.fold_in(key_list[6], part), 71), part)
    member_order = draw_member_order(jax.random.fold_in(jax.random.fold_in(key_list[6], part), 71), part)
    owner_map = draw_owner_map(jax.random.fold_in(jax.random.fold_in(key_list[6], part), 71), part)
    counts = draw_counts(jax.random.fold_in(jax.random.fold_in(key_list[6], part), 71), part)
    return dict(embeddings=embeddings, basis=basis, cluster_ids=cluster_ids, member_order=member_order, owner_map=owner_map, counts=counts)


epsilon = 1e-06

def normalize(rows, basis):
    projected = jnp.dot(rows, basis, preferred_element_type=jnp.float32)
    scale = lax.rsqrt(lax.optimization_barrier(jnp.sum(projected * projected, axis=1, keepdims=True)) + epsilon)
    return (projected * scale).astype(jnp.bfloat16)

def reference(embeddings, basis, cluster_ids, member_order, owner_map, counts):
    normalized = normalize(embeddings, basis)
    doc_total = normalized.shape[0]
    width = normalized.shape[1]
    cluster_total = owner_map.shape[0]
    window = N_ROW * CAP
    block_rows = min(512, doc_total)
    sort_keys = (cluster_ids * doc_total + member_order).astype(jnp.int32)
    ordering = jnp.argsort(sort_keys)
    sorted_vectors = normalized[ordering]
    sorted_groups = cluster_ids[ordering]
    sorted_orders = member_order[ordering]
    padded_vectors = jnp.concatenate([jnp.zeros((window, width), normalized.dtype), sorted_vectors], axis=0)
    padded_groups = jnp.concatenate([jnp.full((window,), -1, jnp.int32), sorted_groups.astype(jnp.int32)], axis=0)
    padded_orders = jnp.concatenate([jnp.zeros((window,), jnp.int32), sorted_orders.astype(jnp.int32)], axis=0)

    def one_block(start):
        queries = lax.dynamic_slice_in_dim(sorted_vectors, start, block_rows)
        query_groups = lax.dynamic_slice_in_dim(sorted_groups, start, block_rows)
        query_orders = lax.dynamic_slice_in_dim(sorted_orders, start, block_rows)
        keys = lax.dynamic_slice_in_dim(padded_vectors, start, window + block_rows)
        key_groups = lax.dynamic_slice_in_dim(padded_groups, start, window + block_rows)
        key_orders = lax.dynamic_slice_in_dim(padded_orders, start, window + block_rows)
        scores = jnp.dot(queries, keys.T, preferred_element_type=jnp.float32)
        allowed = (key_groups[None, :] == query_groups[:, None]) & (key_orders[None, :] < query_orders[:, None])
        return lax.optimization_barrier(jnp.max(jnp.where(allowed, scores, jnp.float32(-1.0)), axis=1))
    starts = jnp.arange(doc_total // block_rows, dtype=jnp.int32) * block_rows
    sorted_best = lax.map(one_block, starts).reshape(-1)
    best = jnp.zeros((doc_total,), jnp.float32).at[ordering].set(sorted_best)
    contrib = jnp.where(member_order >= 1, best, jnp.float32(0.0))
    cluster_sum = jax.ops.segment_sum(contrib, cluster_ids, num_segments=cluster_total)
    cluster_mean = cluster_sum / counts.astype(jnp.float32)
    owned_order = jnp.argsort((owner_map * cluster_total + jnp.arange(cluster_total, dtype=jnp.int32)).astype(jnp.int32))
    cluster_scores = cluster_mean[owned_order]
    return (best, cluster_scores)
```

```python
import functools

import jax
import jax.numpy as jnp
from jax import lax
from jax.experimental import pallas as pl
from jax.experimental.pallas import tpu as pltpu
from jax.sharding import PartitionSpec as P

epsilon = 1e-06
MESH = pl.DeviceIdType.MESH
CHUNKS = 2


def row_of(tile, reduce):
    pieces = [
        reduce(jnp.transpose(tile[i : i + 128, :]), axis=0, keepdims=True)
        for i in range(0, tile.shape[0], 128)
    ]
    return pieces[0] if len(pieces) == 1 else jnp.concatenate(pieces, axis=1)


def kernel(
    n, lines, emb_hbm, basis_hbm, meta_ref, owner_ref,
    best_ref, scores_ref,
    emb, basis, blk, meta, kcol, ccol, acc, col, row, home, rr, rc, part,
    load_sem, basis_sem, own_send, plane_recv, fwd_plane, line_recv, fwd_send,
    meta_send, meta_recv, row_send, row_recv, col_send, col_recv, part_send, part_recv,
):
    planes = n // lines
    half = planes // 2
    docs = blk.shape[1]
    size = docs // CHUNKS
    clusters = owner_ref.shape[1]
    order_bits = (n * docs - 1).bit_length()
    group_of = lambda keys: lax.shift_right_logical(keys, order_bits)
    me = lax.axis_index("row")
    z = me // lines
    line = me % lines

    def from_below(s, at):
        return (s >= 0) & (s < half) & (s < at) & (at <= planes - 2)

    def from_above(s, at):
        return (s < planes) & (at < s) & (at >= 0) & ((s == planes - 1) | ((s >= half) & (at >= half)))

    def piece(d, c):
        return blk.at[d, pl.ds(c * size, size)]

    def remote(src, dst, send, recv, device):
        return pltpu.make_async_remote_copy(
            src_ref=src, dst_ref=dst, send_sem=send, recv_sem=recv,
            device_id={"row": device}, device_id_type=MESH,
        )

    def block_copy(d, c, send, recv, device):
        return remote(piece(d, c), piece(d, c), send, recv, device)

    basis_copy = pltpu.make_async_copy(basis_hbm, basis, basis_sem)
    basis_copy.start()
    loads = []
    for c in range(CHUNKS):
        part_rows = pl.ds(c * size, size)
        load = pltpu.make_async_copy(emb_hbm.at[part_rows], emb.at[part_rows], load_sem.at[c])
        load.start()
        loads.append(load)

    barrier = pltpu.get_barrier_semaphore()

    @pl.loop(1, n)
    def _(k):
        pl.semaphore_signal(barrier, inc=1, device_id={"row": (me + k) % n}, device_id_type=MESH)

    pl.semaphore_wait(barrier, n - 1)

    meta[me] = meta_ref[...]

    def meta_copy(k):
        return remote(meta.at[me], meta.at[me], meta_send.at[k], meta_recv.at[me], (me + k) % n)

    @pl.loop(1, n)
    def _(k):
        meta_copy(k).start()

    goes_up = from_below(z, z + 1)
    goes_down = from_above(z, z - 1)

    def own_copies(c):
        copies = [(None, block_copy(me, c, own_send.at[0, c], plane_recv.at[line, c], me ^ 1))]
        if lines == 4:
            copies.append((None, block_copy(me, c, own_send.at[1, c], plane_recv.at[line, c], me ^ 2)))
        if planes > 1:
            up = jnp.minimum(me + lines, n - 1)
            down = jnp.maximum(me - lines, 0)
            copies.append((goes_up, block_copy(me, c, own_send.at[2, c], line_recv.at[z, c], up)))
            copies.append((goes_down, block_copy(me, c, own_send.at[3, c], line_recv.at[z, c], down)))
        return copies

    def each(copies, act):
        for condition, copy in copies:
            if condition is None:
                act(copy)
            else:
                pl.when(condition)(functools.partial(act, copy))

    basis_copy.wait()
    for c in range(CHUNKS):
        loads[c].wait()
        projected = jnp.dot(
            emb[pl.ds(c * size, size), :], basis[...], preferred_element_type=jnp.float32
        )
        scale = lax.rsqrt(jnp.sum(projected * projected, axis=1, keepdims=True) + epsilon)
        blk[me, pl.ds(c * size, size), :] = (projected * scale).astype(jnp.bfloat16)
        each(own_copies(c)[::-1], lambda copy: copy.start())

    @pl.loop(1, n)
    def _(k):
        d = (me + k) % n
        remote(meta.at[d], meta.at[d], meta_send.at[k], meta_recv.at[d], d).wait_recv()

    for p in range(lines):
        keys = meta[z * lines + p][:, :docs]
        for i in range(0, docs, 128):
            column = jnp.transpose(jnp.broadcast_to(keys[:, i : i + 128], (128, 128)))
            kcol[pl.ds(p * docs + i, 128), :] = column
            ccol[pl.ds(p * docs + i, 128), :] = group_of(column)
    acc[...] = jnp.full_like(acc, -1.0)

    def plane_wait(p, c):
        block_copy(z * lines + p, c, own_send.at[0, c], plane_recv.at[p, c], me ^ 1).wait_recv()

    def line_wait(s, c):
        block_copy(s * lines + line, c, own_send.at[0, c], line_recv.at[s, c], me ^ 1).wait_recv()

    def forward(s, c, device):
        return block_copy(s * lines + line, c, fwd_send.at[s, c], line_recv.at[s, c], device)

    def arrivals(k):
        low, high = z - k, z + k
        below = from_below(low, z)
        above = from_above(high, z)
        return (
            (jnp.maximum(low, 0), below, below & from_below(low, z + 1), jnp.minimum(me + lines, n - 1)),
            (jnp.minimum(high, planes - 1), above, above & from_above(high, z - 1), jnp.maximum(me - lines, 0)),
        )

    def forward_step(k, c):
        for s, _, on, device in arrivals(k):
            @pl.when(on)
            def _():
                line_wait(s, c)
                forward(s, c, device).start()

    def diagonal_copy(c):
        return block_copy(me ^ 2, c, fwd_plane.at[c], plane_recv.at[line ^ 2, c], me ^ 1)

    for c in range(CHUNKS):
        forward_step(1, c)
        if lines == 4:
            plane_wait(line ^ 2, c)
            diagonal_copy(c).start()
    for c in range(CHUNKS):
        plane_wait(line ^ 1, c)
        if lines == 4:
            plane_wait(line ^ 3, c)

    def process(d, s, c, visitor):
        keys = blk[d, pl.ds(c * size, size), :]
        at = pl.ds(pl.multiple_of(c * size, size), size)
        lane_keys = meta[d, :, at]
        lane_groups = group_of(lane_keys)

        def one(p, carry):
            scores = lax.dot_general(
                blk[z * lines + p], keys, (((1,), (1,)), ((), ())), preferred_element_type=jnp.float32
            )
            rows = pl.ds(pl.multiple_of(p * docs, docs), docs)
            k_col, c_col = kcol[rows, :], ccol[rows, :]
            row_part = acc[rows, :] if visitor else None
            outs = []
            for i in range(0, size, 128):
                lk, lg = lane_keys[:, i : i + 128], lane_groups[:, i : i + 128]
                s_same = jnp.where(c_col == lg, scores[:, i : i + 128], -1.0)
                if visitor:
                    earlier = lk < k_col
                    row_part = jnp.maximum(row_part, jnp.where(earlier, s_same, -1.0))
                    for_lane = jnp.where(earlier, -1.0, s_same)
                else:
                    for_lane = jnp.where(k_col < lk, s_same, -1.0)
                outs.append(jnp.max(for_lane, axis=0, keepdims=True))
            if visitor:
                acc[rows, :] = row_part
            return jnp.maximum(carry, jnp.concatenate(outs, axis=1))

        result = lax.fori_loop(0, lines, one, jnp.full((1, size), -1.0, jnp.float32))
        if visitor:
            col[s, :, at] = result
        else:
            home[:, at] = result

    def col_copy(s, at, device):
        return remote(col.at[s], rc.at[at], col_send.at[s], col_recv.at[at], device)

    def process_step(k):
        for s, here, on, _ in arrivals(k):
            @pl.when(here)
            def _():
                @pl.loop(0, CHUNKS)
                def _(c):
                    @pl.when(jnp.logical_not(on))
                    def _():
                        line_wait(s, c)
                    process(s * lines + line, s, c, True)
                col_copy(s, z, s * lines + line).start()

    if planes > 2:
        forward_step(2, 0)

    @pl.loop(0, CHUNKS)
    def _(c):
        process(me, z, c, False)

    if planes > 2:
        for c in range(1, CHUNKS):
            forward_step(2, c)
    if planes > 1:
        process_step(1)

        @pl.loop(2, planes)
        def _(k):
            for c in range(CHUNKS):
                forward_step(k + 1, c)
            process_step(k)

    for p in range(lines):
        row[p] = row_of(acc[p * docs : (p + 1) * docs, :], jnp.max)

    def row_copy(q):
        return remote(row.at[line ^ q], rr.at[line], row_send.at[q], row_recv.at[line], me ^ q)

    for q in range(1, lines):
        row_copy(q).start()
    home[...] = jnp.maximum(home[...], row[line])
    for q in range(1, lines):
        remote(row.at[line], rr.at[line ^ q], row_send.at[q], row_recv.at[line ^ q], me ^ q).wait_recv()
        home[...] = jnp.maximum(home[...], rr[line ^ q])

    @pl.loop(0, planes)
    def _(at):
        @pl.when(from_below(z, at) | from_above(z, at))
        def _():
            remote(col.at[z], rc.at[at], col_send.at[z], col_recv.at[at], me ^ 1).wait_recv()
            home[...] = jnp.maximum(home[...], rc[at])

    best = home[...]
    best_ref[...] = best

    own_keys = meta[me][:, :docs]
    own_groups = group_of(own_keys)
    adds = jnp.where(own_keys - lax.shift_left(own_groups, order_bits) >= 1, best, 0.0)
    for i in range(0, clusters, 128):
        ids = lax.broadcasted_iota(jnp.int32, (128, 128), 0) + i
        total = jnp.zeros((128, 128), jnp.float32)
        for j in range(0, docs, 128):
            total += jnp.where(ids == own_groups[:, j : j + 128], adds[:, j : j + 128], 0.0)
        part[me, :, i : i + 128] = row_of(total, jnp.sum)

    def part_copy(k):
        return remote(part.at[me], part.at[me], part_send.at[k], part_recv.at[me], (me + k) % n)

    @pl.loop(1, n)
    def _(k):
        part_copy(k).start()

    owned = (owner_ref[...] == me).astype(jnp.float32)
    before = (
        lax.broadcasted_iota(jnp.int32, (clusters, clusters), 0)
        < lax.broadcasted_iota(jnp.int32, (clusters, clusters), 1)
    ).astype(jnp.bfloat16)
    per_owner = clusters // n
    many = jnp.broadcast_to(owned, (per_owner, clusters))
    rank = jnp.dot(many.astype(jnp.bfloat16), before, preferred_element_type=jnp.float32)
    wanted = lax.broadcasted_iota(jnp.int32, (per_owner, clusters), 0).astype(jnp.float32)
    pick = (many > 0.5) & (rank == wanted)

    @pl.loop(1, n)
    def _(k):
        d = (me + k) % n
        remote(part.at[d], part.at[d], part_send.at[k], part_recv.at[d], d).wait_recv()

    sums = jnp.zeros((1, clusters), jnp.float32)
    counts = jnp.zeros((1, clusters), jnp.int32)
    for d in range(n):
        sums += part[d]
        counts += meta[d][:, docs:]
    mean = sums / counts.astype(jnp.float32)
    scores_ref[...] = jnp.sum(jnp.where(pick, mean, 0.0), axis=1, keepdims=True)

    for c in range(CHUNKS):
        each(own_copies(c), lambda copy: copy.wait_send())
        if lines == 4:
            diagonal_copy(c).wait_send()

    @pl.loop(1, n)
    def _(k):
        meta_copy(k).wait_send()
        part_copy(k).wait_send()

    for q in range(1, lines):
        row_copy(q).wait_send()

    @pl.loop(1, planes)
    def _(k):
        for s, here, on, device in arrivals(k):
            @pl.when(here)
            def _():
                col_copy(s, z, s * lines + line).wait_send()

            @pl.when(on)
            def _():
                for c in range(CHUNKS):
                    forward(s, c, device).wait_send()


def body(embeddings, basis, cluster_ids, member_order, owner_map, counts):
    n = lax.axis_size("row")
    docs, width = embeddings.shape
    kept = basis.shape[1]
    clusters = owner_map.shape[0]
    lines = 4 if n <= 16 else 2
    planes = n // lines
    share = counts.shape[0]
    lane = lax.iota(jnp.int32, clusters)
    placed = jnp.where(lane // share == lax.axis_index("row"), jnp.tile(counts, n), 0)
    meta = jnp.concatenate([(cluster_ids << (n * docs - 1).bit_length()) + member_order, placed]).reshape(1, -1)
    vmem = functools.partial(pl.BlockSpec, memory_space=pltpu.VMEM)
    hbm = functools.partial(pl.BlockSpec, memory_space=pl.ANY)
    dma = pltpu.SemaphoreType.DMA
    f32, i32, bf16 = jnp.float32, jnp.int32, jnp.bfloat16
    best, scores = pl.pallas_call(
        functools.partial(kernel, n, lines),
        out_shape=(
            jax.ShapeDtypeStruct((1, docs), f32),
            jax.ShapeDtypeStruct((clusters // n, 1), f32),
        ),
        in_specs=[hbm(), hbm(), vmem(), vmem()],
        out_specs=(vmem(), vmem()),
        scratch_shapes=[
            pltpu.VMEM((docs, width), bf16),
            pltpu.VMEM((width, kept), bf16),
            pltpu.VMEM((n, docs, kept), bf16),
            pltpu.VMEM((n, 1, docs + clusters), i32),
            pltpu.VMEM((lines * docs, 128), i32),
            pltpu.VMEM((lines * docs, 128), i32),
            pltpu.VMEM((lines * docs, 128), f32),
            pltpu.VMEM((planes, 1, docs), f32),
            pltpu.VMEM((lines, 1, docs), f32),
            pltpu.VMEM((1, docs), f32),
            pltpu.VMEM((lines, 1, docs), f32),
            pltpu.VMEM((planes, 1, docs), f32),
            pltpu.VMEM((n, 1, clusters), f32),
            dma((CHUNKS,)),
            dma,
            dma((4, CHUNKS)),
            dma((lines, CHUNKS)),
            dma((CHUNKS,)),
            dma((planes, CHUNKS)),
            dma((planes, CHUNKS)),
            dma((n,)),
            dma((n,)),
            dma((lines,)),
            dma((lines,)),
            dma((planes,)),
            dma((planes,)),
            dma((n,)),
            dma((n,)),
        ],
        compiler_params=pltpu.CompilerParams(
            collective_id=0, has_side_effects=True, vmem_limit_bytes=48 * 1024 * 1024
        ),
        name="cluster_scores",
    )(embeddings, basis, meta, owner_map.reshape(1, -1))
    return best.reshape(-1), scores.reshape(-1)


def solution(mesh):
    in_specs = (
        P(("groups", "row"), None),
        P(),
        P(("groups", "row")),
        P(("groups", "row")),
        P("groups"),
        P(("groups", "row")),
    )
    out_specs = (P(("groups", "row")), P(("groups", "row")))
    return jax.shard_map(body, mesh=mesh, in_specs=in_specs, out_specs=out_specs, check_vma=False)
```

```python
import functools

import jax
import jax.numpy as jnp
from jax import lax
from jax.experimental import pallas as pl
from jax.experimental.pallas import tpu as pltpu
from jax.sharding import PartitionSpec as P

epsilon = 1e-06
MESH = pl.DeviceIdType.MESH
CHUNKS = 2


def row_of(tile, reduce):
    pieces = [
        reduce(jnp.transpose(tile[i : i + 128, :]), axis=0, keepdims=True)
        for i in range(0, tile.shape[0], 128)
    ]
    return pieces[0] if len(pieces) == 1 else jnp.concatenate(pieces, axis=1)


def kernel(
    n, lines, emb_hbm, basis_hbm, ids_hbm, order_hbm, owner_hbm, counts_hbm,
    best_ref, scores_ref,
    ids, order, owner, counts_here, emb, basis, blk, meta, kcol, ccol, acc, col, row, home, rr, rc, part,
    small_sem, load_sem, basis_sem, own_send, plane_recv, fwd_plane, line_recv, fwd_send,
    meta_send, meta_recv, row_send, row_recv, col_send, col_recv, part_send, part_recv,
):
    planes = n // lines
    half = planes // 2
    docs = blk.shape[1]
    size = docs // CHUNKS
    clusters = owner_hbm.shape[0]
    share = counts_hbm.shape[0]
    order_bits = (n * docs - 1).bit_length()
    group_of = lambda keys: lax.shift_right_logical(keys, order_bits)
    me = lax.axis_index("row")
    z = me // lines
    line = me % lines

    def from_below(s, at):
        return (s >= 0) & (s < half) & (s < at) & (at <= planes - 2)

    def from_above(s, at):
        return (s < planes) & (at < s) & (at >= 0) & ((s == planes - 1) | ((s >= half) & (at >= half)))

    def piece(d, c):
        return blk.at[d, pl.ds(c * size, size)]

    def remote(src, dst, send, recv, device):
        return pltpu.make_async_remote_copy(
            src_ref=src, dst_ref=dst, send_sem=send, recv_sem=recv,
            device_id={"row": device}, device_id_type=MESH,
        )

    def block_copy(d, c, send, recv, device):
        return remote(piece(d, c), piece(d, c), send, recv, device)

    smalls = [
        pltpu.make_async_copy(source, target, small_sem.at[i])
        for i, (source, target) in enumerate(
            ((ids_hbm, ids), (order_hbm, order), (owner_hbm, owner), (counts_hbm, counts_here))
        )
    ]
    for copy in smalls:
        copy.start()
    basis_copy = pltpu.make_async_copy(basis_hbm, basis, basis_sem)
    basis_copy.start()
    loads = []
    for c in range(CHUNKS):
        part_rows = pl.ds(c * size, size)
        load = pltpu.make_async_copy(emb_hbm.at[part_rows], emb.at[part_rows], load_sem.at[c])
        load.start()
        loads.append(load)

    barrier = pltpu.get_barrier_semaphore()

    @pl.loop(1, n)
    def _(k):
        pl.semaphore_signal(barrier, inc=1, device_id={"row": (me + k) % n}, device_id_type=MESH)

    pl.semaphore_wait(barrier, n - 1)

    for copy in smalls:
        copy.wait()
    own_ids = ids[...].reshape(1, docs)
    own_order = order[...].reshape(1, docs)
    meta[me, :, :docs] = lax.shift_left(own_ids, order_bits) + own_order
    lane = lax.broadcasted_iota(jnp.int32, (1, clusters), 1) - me * share
    placed = jnp.zeros((1, clusters), jnp.int32)
    for k in range(share):
        placed = jnp.where(lane == k, counts_here[k], placed)
    meta[me, :, docs:] = placed

    def meta_copy(k):
        return remote(meta.at[me], meta.at[me], meta_send.at[k], meta_recv.at[me], (me + k) % n)

    @pl.loop(1, n)
    def _(k):
        meta_copy(k).start()

    goes_up = from_below(z, z + 1)
    goes_down = from_above(z, z - 1)

    def own_copies(c):
        copies = [(None, block_copy(me, c, own_send.at[0, c], plane_recv.at[line, c], me ^ 1))]
        if lines == 4:
            copies.append((None, block_copy(me, c, own_send.at[1, c], plane_recv.at[line, c], me ^ 2)))
        if planes > 1:
            up = jnp.minimum(me + lines, n - 1)
            down = jnp.maximum(me - lines, 0)
            copies.append((goes_up, block_copy(me, c, own_send.at[2, c], line_recv.at[z, c], up)))
            copies.append((goes_down, block_copy(me, c, own_send.at[3, c], line_recv.at[z, c], down)))
        return copies

    def each(copies, act):
        for condition, copy in copies:
            if condition is None:
                act(copy)
            else:
                pl.when(condition)(functools.partial(act, copy))

    basis_copy.wait()
    for c in range(CHUNKS):
        loads[c].wait()
        projected = jnp.dot(
            emb[pl.ds(c * size, size), :], basis[...], preferred_element_type=jnp.float32
        )
        scale = lax.rsqrt(jnp.sum(projected * projected, axis=1, keepdims=True) + epsilon)
        blk[me, pl.ds(c * size, size), :] = (projected * scale).astype(jnp.bfloat16)
        each(own_copies(c)[::-1], lambda copy: copy.start())

    @pl.loop(1, n)
    def _(k):
        d = (me + k) % n
        remote(meta.at[d], meta.at[d], meta_send.at[k], meta_recv.at[d], d).wait_recv()

    for p in range(lines):
        keys = meta[z * lines + p][:, :docs]
        for i in range(0, docs, 128):
            column = jnp.transpose(jnp.broadcast_to(keys[:, i : i + 128], (128, 128)))
            kcol[pl.ds(p * docs + i, 128), :] = column
            ccol[pl.ds(p * docs + i, 128), :] = group_of(column)
    acc[...] = jnp.full_like(acc, -1.0)

    def plane_wait(p, c):
        block_copy(z * lines + p, c, own_send.at[0, c], plane_recv.at[p, c], me ^ 1).wait_recv()

    def line_wait(s, c):
        block_copy(s * lines + line, c, own_send.at[0, c], line_recv.at[s, c], me ^ 1).wait_recv()

    def forward(s, c, device):
        return block_copy(s * lines + line, c, fwd_send.at[s, c], line_recv.at[s, c], device)

    def arrivals(k):
        low, high = z - k, z + k
        below = from_below(low, z)
        above = from_above(high, z)
        return (
            (jnp.maximum(low, 0), below, below & from_below(low, z + 1), jnp.minimum(me + lines, n - 1)),
            (jnp.minimum(high, planes - 1), above, above & from_above(high, z - 1), jnp.maximum(me - lines, 0)),
        )

    def forward_step(k, c):
        for s, _, on, device in arrivals(k):
            @pl.when(on)
            def _():
                line_wait(s, c)
                forward(s, c, device).start()

    def diagonal_copy(c):
        return block_copy(me ^ 2, c, fwd_plane.at[c], plane_recv.at[line ^ 2, c], me ^ 1)

    for c in range(CHUNKS):
        forward_step(1, c)
        if lines == 4:
            plane_wait(line ^ 2, c)
            diagonal_copy(c).start()
    for c in range(CHUNKS):
        plane_wait(line ^ 1, c)
        if lines == 4:
            plane_wait(line ^ 3, c)

    def process(d, s, c, visitor):
        keys = blk[d, pl.ds(c * size, size), :]
        at = pl.ds(pl.multiple_of(c * size, size), size)
        lane_keys = meta[d, :, at]
        lane_groups = group_of(lane_keys)

        def one(p, carry):
            scores = lax.dot_general(
                blk[z * lines + p], keys, (((1,), (1,)), ((), ())), preferred_element_type=jnp.float32
            )
            rows = pl.ds(pl.multiple_of(p * docs, docs), docs)
            k_col, c_col = kcol[rows, :], ccol[rows, :]
            row_part = acc[rows, :] if visitor else None
            outs = []
            for i in range(0, size, 128):
                lk, lg = lane_keys[:, i : i + 128], lane_groups[:, i : i + 128]
                s_same = jnp.where(c_col == lg, scores[:, i : i + 128], -1.0)
                if visitor:
                    earlier = lk < k_col
                    row_part = jnp.maximum(row_part, jnp.where(earlier, s_same, -1.0))
                    for_lane = jnp.where(earlier, -1.0, s_same)
                else:
                    for_lane = jnp.where(k_col < lk, s_same, -1.0)
                outs.append(jnp.max(for_lane, axis=0, keepdims=True))
            if visitor:
                acc[rows, :] = row_part
            return jnp.maximum(carry, jnp.concatenate(outs, axis=1))

        result = lax.fori_loop(0, lines, one, jnp.full((1, size), -1.0, jnp.float32))
        if visitor:
            col[s, :, at] = result
        else:
            home[:, at] = result

    def col_copy(s, at, device):
        return remote(col.at[s], rc.at[at], col_send.at[s], col_recv.at[at], device)

    def process_step(k):
        for s, here, on, _ in arrivals(k):
            @pl.when(here)
            def _():
                @pl.loop(0, CHUNKS)
                def _(c):
                    @pl.when(jnp.logical_not(on))
                    def _():
                        line_wait(s, c)
                    process(s * lines + line, s, c, True)
                col_copy(s, z, s * lines + line).start()

    if planes > 2:
        forward_step(2, 0)

    @pl.loop(0, CHUNKS)
    def _(c):
        process(me, z, c, False)

    if planes > 2:
        for c in range(1, CHUNKS):
            forward_step(2, c)
    if planes > 1:
        process_step(1)

        @pl.loop(2, planes)
        def _(k):
            for c in range(CHUNKS):
                forward_step(k + 1, c)
            process_step(k)

    for p in range(lines):
        row[p] = row_of(acc[p * docs : (p + 1) * docs, :], jnp.max)

    def row_copy(q):
        return remote(row.at[line ^ q], rr.at[line], row_send.at[q], row_recv.at[line], me ^ q)

    for q in range(1, lines):
        row_copy(q).start()
    home[...] = jnp.maximum(home[...], row[line])
    for q in range(1, lines):
        remote(row.at[line], rr.at[line ^ q], row_send.at[q], row_recv.at[line ^ q], me ^ q).wait_recv()
        home[...] = jnp.maximum(home[...], rr[line ^ q])

    @pl.loop(0, planes)
    def _(at):
        @pl.when(from_below(z, at) | from_above(z, at))
        def _():
            remote(col.at[z], rc.at[at], col_send.at[z], col_recv.at[at], me ^ 1).wait_recv()
            home[...] = jnp.maximum(home[...], rc[at])

    best = home[...]
    best_ref[...] = best

    adds = jnp.where(own_order >= 1, best, 0.0)
    for i in range(0, clusters, 128):
        ids_row = lax.broadcasted_iota(jnp.int32, (128, 128), 0) + i
        total = jnp.zeros((128, 128), jnp.float32)
        for j in range(0, docs, 128):
            total += jnp.where(ids_row == own_ids[:, j : j + 128], adds[:, j : j + 128], 0.0)
        part[me, :, i : i + 128] = row_of(total, jnp.sum)

    def part_copy(k):
        return remote(part.at[me], part.at[me], part_send.at[k], part_recv.at[me], (me + k) % n)

    @pl.loop(1, n)
    def _(k):
        part_copy(k).start()

    owned = (owner[...].reshape(1, clusters) == me).astype(jnp.float32)
    before = (
        lax.broadcasted_iota(jnp.int32, (clusters, clusters), 0)
        < lax.broadcasted_iota(jnp.int32, (clusters, clusters), 1)
    ).astype(jnp.bfloat16)
    per_owner = clusters // n
    many = jnp.broadcast_to(owned, (per_owner, clusters))
    rank = jnp.dot(many.astype(jnp.bfloat16), before, preferred_element_type=jnp.float32)
    wanted = lax.broadcasted_iota(jnp.int32, (per_owner, clusters), 0).astype(jnp.float32)
    pick = (many > 0.5) & (rank == wanted)

    @pl.loop(1, n)
    def _(k):
        d = (me + k) % n
        remote(part.at[d], part.at[d], part_send.at[k], part_recv.at[d], d).wait_recv()

    sums = jnp.zeros((1, clusters), jnp.float32)
    counts = jnp.zeros((1, clusters), jnp.int32)
    for d in range(n):
        sums += part[d]
        counts += meta[d][:, docs:]
    mean = sums / counts.astype(jnp.float32)
    picked = jnp.where(pick, mean, 0.0)
    folded = sum(picked[:, i : i + 128] for i in range(0, clusters, 128))
    rest = jnp.zeros((128 - per_owner, 128), jnp.float32)
    scores_ref[...] = row_of(jnp.concatenate([folded, rest], axis=0), jnp.sum)[:, :per_owner]

    for c in range(CHUNKS):
        each(own_copies(c), lambda copy: copy.wait_send())
        if lines == 4:
            diagonal_copy(c).wait_send()

    @pl.loop(1, n)
    def _(k):
        meta_copy(k).wait_send()
        part_copy(k).wait_send()

    for q in range(1, lines):
        row_copy(q).wait_send()

    @pl.loop(1, planes)
    def _(k):
        for s, here, on, device in arrivals(k):
            @pl.when(here)
            def _():
                col_copy(s, z, s * lines + line).wait_send()

            @pl.when(on)
            def _():
                for c in range(CHUNKS):
                    forward(s, c, device).wait_send()


def body(embeddings, basis, cluster_ids, member_order, owner_map, counts):
    n = lax.axis_size("row")
    docs, width = embeddings.shape
    kept = basis.shape[1]
    clusters = owner_map.shape[0]
    lines = 4 if n <= 16 else 2
    planes = n // lines
    share = counts.shape[0]
    vmem = functools.partial(pl.BlockSpec, memory_space=pltpu.VMEM)
    hbm = functools.partial(pl.BlockSpec, memory_space=pl.ANY)
    dma = pltpu.SemaphoreType.DMA
    f32, i32, bf16 = jnp.float32, jnp.int32, jnp.bfloat16
    best, scores = pl.pallas_call(
        functools.partial(kernel, n, lines),
        out_shape=(
            jax.ShapeDtypeStruct((1, docs), f32),
            jax.ShapeDtypeStruct((1, clusters // n), f32),
        ),
        in_specs=[hbm()] * 6,
        out_specs=(vmem(), vmem()),
        scratch_shapes=[
            pltpu.VMEM((docs,), i32),
            pltpu.VMEM((docs,), i32),
            pltpu.VMEM((clusters,), i32),
            pltpu.SMEM((share,), i32),
            pltpu.VMEM((docs, width), bf16),
            pltpu.VMEM((width, kept), bf16),
            pltpu.VMEM((n, docs, kept), bf16),
            pltpu.VMEM((n, 1, docs + clusters), i32),
            pltpu.VMEM((lines * docs, 128), i32),
            pltpu.VMEM((lines * docs, 128), i32),
            pltpu.VMEM((lines * docs, 128), f32),
            pltpu.VMEM((planes, 1, docs), f32),
            pltpu.VMEM((lines, 1, docs), f32),
            pltpu.VMEM((1, docs), f32),
            pltpu.VMEM((lines, 1, docs), f32),
            pltpu.VMEM((planes, 1, docs), f32),
            pltpu.VMEM((n, 1, clusters), f32),
            dma((4,)),
            dma((CHUNKS,)),
            dma,
            dma((4, CHUNKS)),
            dma((lines, CHUNKS)),
            dma((CHUNKS,)),
            dma((planes, CHUNKS)),
            dma((planes, CHUNKS)),
            dma((n,)),
            dma((n,)),
            dma((lines,)),
            dma((lines,)),
            dma((planes,)),
            dma((planes,)),
            dma((n,)),
            dma((n,)),
        ],
        compiler_params=pltpu.CompilerParams(
            collective_id=0, has_side_effects=True, vmem_limit_bytes=63 * 1024 * 1024
        ),
        name="cluster_scores",
    )(embeddings, basis, cluster_ids, member_order, owner_map, counts)
    return best.reshape(-1), scores.reshape(-1)


def solution(mesh):
    in_specs = (
        P(("groups", "row"), None),
        P(),
        P(("groups", "row")),
        P(("groups", "row")),
        P("groups"),
        P(("groups", "row")),
    )
    out_specs = (P(("groups", "row")), P(("groups", "row")))
    return jax.shard_map(body, mesh=mesh, in_specs=in_specs, out_specs=out_specs, check_vma=False)
```

```python
import functools

import jax
import jax.numpy as jnp
from jax import lax
from jax.experimental import pallas as pl
from jax.experimental.pallas import tpu as pltpu
from jax.sharding import PartitionSpec as P

epsilon = 1e-06
MESH = pl.DeviceIdType.MESH
CHUNKS = 2


def row_of(tile, reduce):
    pieces = [
        reduce(jnp.transpose(tile[i : i + 128, :]), axis=0, keepdims=True)
        for i in range(0, tile.shape[0], 128)
    ]
    return pieces[0] if len(pieces) == 1 else jnp.concatenate(pieces, axis=1)


def kernel(
    n, lines, emb_hbm, basis_hbm, ids_hbm, order_hbm, owner_hbm, counts_hbm,
    best_ref, scores_ref,
    ids, order, owner, counts_here, emb, basis, blk, meta, kcol, ccol, acc, col, row, home, rr, rc, plane_part, line_part,
    small_sem, load_sem, basis_sem, own_send, plane_recv, fwd_plane, line_recv, fwd_send,
    meta_send, meta_recv, row_send, row_recv, col_send, col_recv, part_send, part_recv,
):
    planes = n // lines
    half = planes // 2
    docs = blk.shape[1]
    size = docs // CHUNKS
    clusters = owner_hbm.shape[0]
    share = counts_hbm.shape[0]
    order_bits = (n * docs - 1).bit_length()
    group_of = lambda keys: lax.shift_right_logical(keys, order_bits)
    me = lax.axis_index("row")
    z = me // lines
    line = me % lines

    def from_below(s, at):
        return (s >= 0) & (s < half) & (s < at) & (at <= planes - 2)

    def from_above(s, at):
        return (s < planes) & (at < s) & (at >= 0) & ((s == planes - 1) | ((s >= half) & (at >= half)))

    def piece(d, c):
        return blk.at[d, pl.ds(c * size, size)]

    def remote(src, dst, send, recv, device):
        return pltpu.make_async_remote_copy(
            src_ref=src, dst_ref=dst, send_sem=send, recv_sem=recv,
            device_id={"row": device}, device_id_type=MESH,
        )

    def block_copy(d, c, send, recv, device):
        return remote(piece(d, c), piece(d, c), send, recv, device)

    smalls = [
        pltpu.make_async_copy(source, target, small_sem.at[i])
        for i, (source, target) in enumerate(
            ((ids_hbm, ids), (order_hbm, order), (owner_hbm, owner), (counts_hbm, counts_here))
        )
    ]
    for copy in smalls:
        copy.start()
    basis_copy = pltpu.make_async_copy(basis_hbm, basis, basis_sem)
    basis_copy.start()
    loads = []
    for c in range(CHUNKS):
        part_rows = pl.ds(c * size, size)
        load = pltpu.make_async_copy(emb_hbm.at[part_rows], emb.at[part_rows], load_sem.at[c])
        load.start()
        loads.append(load)

    mates = [(q, me ^ q) for q in range(1, lines)]
    mates += [(lines + k, lax.rem(z + k, planes) * lines + line) for k in range(1, planes)]
    barrier = pltpu.get_barrier_semaphore()
    for _, d in mates:
        pl.semaphore_signal(barrier, inc=1, device_id={"row": d}, device_id_type=MESH)

    def meta_copy(i, d):
        return remote(meta.at[me], meta.at[me], meta_send.at[i], meta_recv.at[me], d)

    goes_up = from_below(z, z + 1)
    goes_down = from_above(z, z - 1)

    def own_copies(c):
        copies = [(None, block_copy(me, c, own_send.at[0, c], plane_recv.at[line, c], me ^ 1))]
        if lines == 4:
            copies.append((None, block_copy(me, c, own_send.at[1, c], plane_recv.at[line, c], me ^ 2)))
        if planes > 1:
            up = jnp.minimum(me + lines, n - 1)
            down = jnp.maximum(me - lines, 0)
            copies.append((goes_up, block_copy(me, c, own_send.at[2, c], line_recv.at[z, c], up)))
            copies.append((goes_down, block_copy(me, c, own_send.at[3, c], line_recv.at[z, c], down)))
        return copies

    def each(copies, act):
        for condition, copy in copies:
            if condition is None:
                act(copy)
            else:
                pl.when(condition)(functools.partial(act, copy))

    basis_copy.wait()
    for c in range(CHUNKS):
        loads[c].wait()
        projected = jnp.dot(
            emb[pl.ds(c * size, size), :], basis[...], preferred_element_type=jnp.float32
        )
        scale = lax.rsqrt(jnp.sum(projected * projected, axis=1, keepdims=True) + epsilon)
        blk[me, pl.ds(c * size, size), :] = (projected * scale).astype(jnp.bfloat16)
        if c == 0:
            pl.semaphore_wait(barrier, len(mates))
        each(own_copies(c)[::-1], lambda copy: copy.start())

    for copy in smalls:
        copy.wait()
    own_ids = ids[...].reshape(1, docs)
    own_order = order[...].reshape(1, docs)
    meta[me] = lax.shift_left(own_ids, order_bits) + own_order
    for i, d in mates:
        meta_copy(i, d).start()
    acc[...] = jnp.full_like(acc, -1.0)
    lane = lax.broadcasted_iota(jnp.int32, (1, clusters), 1) - me * share
    placed = jnp.zeros((1, clusters), jnp.int32)
    for k in range(share):
        placed = jnp.where(lane == k, counts_here[k], placed)
    plane_part[line, :, clusters:] = placed.astype(jnp.float32)

    owned = (owner[...].reshape(1, clusters) == me).astype(jnp.float32)
    before = (
        lax.broadcasted_iota(jnp.int32, (clusters, clusters), 0)
        < lax.broadcasted_iota(jnp.int32, (clusters, clusters), 1)
    ).astype(jnp.bfloat16)
    per_owner = clusters // n
    many = jnp.broadcast_to(owned, (per_owner, clusters))
    rank = jnp.dot(many.astype(jnp.bfloat16), before, preferred_element_type=jnp.float32)
    wanted = lax.broadcasted_iota(jnp.int32, (per_owner, clusters), 0).astype(jnp.float32)
    pick = (many > 0.5) & (rank == wanted)

    for i, d in mates:
        remote(meta.at[d], meta.at[d], meta_send.at[i], meta_recv.at[d], d).wait_recv()

    for p in range(lines):
        keys = meta[z * lines + p]
        for i in range(0, docs, 128):
            column = jnp.transpose(jnp.broadcast_to(keys[:, i : i + 128], (128, 128)))
            kcol[pl.ds(p * docs + i, 128), :] = column
            ccol[pl.ds(p * docs + i, 128), :] = group_of(column)

    def plane_wait(p, c):
        block_copy(z * lines + p, c, own_send.at[0, c], plane_recv.at[p, c], me ^ 1).wait_recv()

    def line_wait(s, c):
        block_copy(s * lines + line, c, own_send.at[0, c], line_recv.at[s, c], me ^ 1).wait_recv()

    def forward(s, c, device):
        return block_copy(s * lines + line, c, fwd_send.at[s, c], line_recv.at[s, c], device)

    def arrivals(k):
        low, high = z - k, z + k
        below = from_below(low, z)
        above = from_above(high, z)
        return (
            (jnp.maximum(low, 0), below, below & from_below(low, z + 1), jnp.minimum(me + lines, n - 1)),
            (jnp.minimum(high, planes - 1), above, above & from_above(high, z - 1), jnp.maximum(me - lines, 0)),
        )

    def forward_step(k, c):
        for s, _, on, device in arrivals(k):
            @pl.when(on)
            def _():
                line_wait(s, c)
                forward(s, c, device).start()

    def diagonal_copy(c):
        return block_copy(me ^ 2, c, fwd_plane.at[c], plane_recv.at[line ^ 2, c], me ^ 1)

    for c in range(CHUNKS):
        forward_step(1, c)
        if lines == 4:
            plane_wait(line ^ 2, c)
            diagonal_copy(c).start()
    for c in range(CHUNKS):
        plane_wait(line ^ 1, c)
        if lines == 4:
            plane_wait(line ^ 3, c)

    def process(d, s, c, visitor):
        keys = blk[d, pl.ds(c * size, size), :]
        at = pl.ds(pl.multiple_of(c * size, size), size)
        lane_keys = meta[d, :, at]
        lane_groups = group_of(lane_keys)

        def one(p, carry):
            scores = lax.dot_general(
                blk[z * lines + p], keys, (((1,), (1,)), ((), ())), preferred_element_type=jnp.float32
            )
            rows = pl.ds(pl.multiple_of(p * docs, docs), docs)
            k_col, c_col = kcol[rows, :], ccol[rows, :]
            row_part = acc[rows, :] if visitor else None
            outs = []
            for i in range(0, size, 128):
                lk, lg = lane_keys[:, i : i + 128], lane_groups[:, i : i + 128]
                s_same = jnp.where(c_col == lg, scores[:, i : i + 128], -1.0)
                if visitor:
                    earlier = lk < k_col
                    row_part = jnp.maximum(row_part, jnp.where(earlier, s_same, -1.0))
                    for_lane = jnp.where(earlier, -1.0, s_same)
                else:
                    for_lane = jnp.where(k_col < lk, s_same, -1.0)
                outs.append(jnp.max(for_lane, axis=0, keepdims=True))
            if visitor:
                acc[rows, :] = row_part
            return jnp.maximum(carry, jnp.concatenate(outs, axis=1))

        result = lax.fori_loop(0, lines, one, jnp.full((1, size), -1.0, jnp.float32))
        if visitor:
            col[s, :, at] = result
        else:
            home[:, at] = result

    def col_copy(s, at, device):
        return remote(col.at[s], rc.at[at], col_send.at[s], col_recv.at[at], device)

    def process_step(k):
        for s, here, on, _ in arrivals(k):
            @pl.when(here)
            def _():
                @pl.loop(0, CHUNKS)
                def _(c):
                    @pl.when(jnp.logical_not(on))
                    def _():
                        line_wait(s, c)
                    process(s * lines + line, s, c, True)
                col_copy(s, z, s * lines + line).start()

    if planes > 2:
        forward_step(2, 0)

    @pl.loop(0, CHUNKS)
    def _(c):
        process(me, z, c, False)

    if planes > 2:
        for c in range(1, CHUNKS):
            forward_step(2, c)
    if planes > 1:
        process_step(1)

        @pl.loop(2, planes)
        def _(k):
            for c in range(CHUNKS):
                forward_step(k + 1, c)
            process_step(k)

    def row_copy(q):
        return remote(row.at[line ^ q], rr.at[line], row_send.at[q], row_recv.at[line], me ^ q)

    for q in [*range(lines - 1, 0, -1), 0]:
        rows = pl.ds(pl.multiple_of((line ^ q) * docs, docs), docs)
        row[line ^ q] = row_of(acc[rows, :], jnp.max)
        if q:
            row_copy(q).start()
    home[...] = jnp.maximum(home[...], row[line])
    for q in range(1, lines):
        remote(row.at[line], rr.at[line ^ q], row_send.at[q], row_recv.at[line ^ q], me ^ q).wait_recv()
        home[...] = jnp.maximum(home[...], rr[line ^ q])

    @pl.loop(0, planes)
    def _(at):
        @pl.when(from_below(z, at) | from_above(z, at))
        def _():
            remote(col.at[z], rc.at[at], col_send.at[z], col_recv.at[at], me ^ 1).wait_recv()
            home[...] = jnp.maximum(home[...], rc[at])

    best = home[...]
    best_ref[...] = best

    adds = jnp.where(own_order >= 1, best, 0.0)
    for i in range(0, clusters, 128):
        ids_row = lax.broadcasted_iota(jnp.int32, (128, 128), 0) + i
        total = jnp.zeros((128, 128), jnp.float32)
        for j in range(0, docs, 128):
            total += jnp.where(ids_row == own_ids[:, j : j + 128], adds[:, j : j + 128], 0.0)
        plane_part[line, :, i : i + 128] = row_of(total, jnp.sum)

    def plane_part_copy(q):
        return remote(
            plane_part.at[line], plane_part.at[line], part_send.at[q], part_recv.at[line], me ^ q
        )

    def line_part_copy(i, d):
        return remote(
            line_part.at[z], line_part.at[z], part_send.at[i], part_recv.at[lines + z], d
        )

    for q in range(lines - 1, 0, -1):
        plane_part_copy(q).start()
    for q in range(1, lines):
        there = plane_part.at[line ^ q]
        remote(there, there, part_send.at[q], part_recv.at[line ^ q], me ^ q).wait_recv()
    line_part[z] = sum(plane_part[p] for p in range(lines))
    for i, d in mates[lines - 1 :]:
        line_part_copy(i, d).start()
    for i, d in mates[lines - 1 :]:
        there = line_part.at[d // lines]
        remote(there, there, part_send.at[i], part_recv.at[lines + d // lines], d).wait_recv()
    totals = sum(line_part[at] for at in range(planes))
    mean = totals[:, :clusters] / totals[:, clusters:]
    picked = jnp.where(pick, mean, 0.0)
    folded = sum(picked[:, i : i + 128] for i in range(0, clusters, 128))
    rest = jnp.zeros((128 - per_owner, 128), jnp.float32)
    scores_ref[...] = row_of(jnp.concatenate([folded, rest], axis=0), jnp.sum)[:, :per_owner]

    for c in range(CHUNKS):
        each(own_copies(c), lambda copy: copy.wait_send())
        if lines == 4:
            diagonal_copy(c).wait_send()

    for i, d in mates:
        meta_copy(i, d).wait_send()
    for q in range(1, lines):
        plane_part_copy(q).wait_send()
    for i, d in mates[lines - 1 :]:
        line_part_copy(i, d).wait_send()

    for q in range(1, lines):
        row_copy(q).wait_send()

    @pl.loop(1, planes)
    def _(k):
        for s, here, on, device in arrivals(k):
            @pl.when(here)
            def _():
                col_copy(s, z, s * lines + line).wait_send()

            @pl.when(on)
            def _():
                for c in range(CHUNKS):
                    forward(s, c, device).wait_send()


def body(embeddings, basis, cluster_ids, member_order, owner_map, counts):
    n = lax.axis_size("row")
    docs, width = embeddings.shape
    kept = basis.shape[1]
    clusters = owner_map.shape[0]
    lines = 4 if n <= 16 else 2
    planes = n // lines
    share = counts.shape[0]
    vmem = functools.partial(pl.BlockSpec, memory_space=pltpu.VMEM)
    hbm = functools.partial(pl.BlockSpec, memory_space=pl.ANY)
    dma = pltpu.SemaphoreType.DMA
    f32, i32, bf16 = jnp.float32, jnp.int32, jnp.bfloat16
    best, scores = pl.pallas_call(
        functools.partial(kernel, n, lines),
        out_shape=(
            jax.ShapeDtypeStruct((1, docs), f32),
            jax.ShapeDtypeStruct((1, clusters // n), f32),
        ),
        in_specs=[hbm()] * 6,
        out_specs=(vmem(), vmem()),
        scratch_shapes=[
            pltpu.VMEM((docs,), i32),
            pltpu.VMEM((docs,), i32),
            pltpu.VMEM((clusters,), i32),
            pltpu.SMEM((share,), i32),
            pltpu.VMEM((docs, width), bf16),
            pltpu.VMEM((width, kept), bf16),
            pltpu.VMEM((n, docs, kept), bf16),
            pltpu.VMEM((n, 1, docs), i32),
            pltpu.VMEM((lines * docs, 128), i32),
            pltpu.VMEM((lines * docs, 128), i32),
            pltpu.VMEM((lines * docs, 128), f32),
            pltpu.VMEM((planes, 1, docs), f32),
            pltpu.VMEM((lines, 1, docs), f32),
            pltpu.VMEM((1, docs), f32),
            pltpu.VMEM((lines, 1, docs), f32),
            pltpu.VMEM((planes, 1, docs), f32),
            pltpu.VMEM((lines, 1, 2 * clusters), f32),
            pltpu.VMEM((planes, 1, 2 * clusters), f32),
            dma((4,)),
            dma((CHUNKS,)),
            dma,
            dma((4, CHUNKS)),
            dma((lines, CHUNKS)),
            dma((CHUNKS,)),
            dma((planes, CHUNKS)),
            dma((planes, CHUNKS)),
            dma((lines + planes,)),
            dma((n,)),
            dma((lines,)),
            dma((lines,)),
            dma((planes,)),
            dma((planes,)),
            dma((lines + planes,)),
            dma((lines + planes,)),
        ],
        compiler_params=pltpu.CompilerParams(
            collective_id=0, has_side_effects=True, vmem_limit_bytes=62 * 1024 * 1024 + 512 * 1024
        ),
        name="cluster_scores",
    )(embeddings, basis, cluster_ids, member_order, owner_map, counts)
    return best.reshape(-1), scores.reshape(-1)


def solution(mesh):
    in_specs = (
        P(("groups", "row"), None),
        P(),
        P(("groups", "row")),
        P(("groups", "row")),
        P("groups"),
        P(("groups", "row")),
    )
    out_specs = (P(("groups", "row")), P(("groups", "row")))
    return jax.shard_map(body, mesh=mesh, in_specs=in_specs, out_specs=out_specs, check_vma=False)
```

```python
import functools

import jax
import jax.numpy as jnp
from jax import lax
from jax.experimental import pallas as pl
from jax.experimental.pallas import tpu as pltpu
from jax.sharding import PartitionSpec as P

epsilon = 1e-06
MESH = pl.DeviceIdType.MESH
CHUNKS = 2


def row_of(tile, reduce):
    pieces = [
        reduce(jnp.transpose(tile[i : i + 128, :]), axis=0, keepdims=True)
        for i in range(0, tile.shape[0], 128)
    ]
    return pieces[0] if len(pieces) == 1 else jnp.concatenate(pieces, axis=1)


def kernel(
    n, lines, emb_hbm, basis_hbm, ids_hbm, order_hbm, owner_hbm, counts_hbm,
    best_ref, scores_ref,
    ids, order, owner, counts_here, emb, basis, blk, meta, kcol, ccol, acc, col, row, home, rr, rc, part,
    small_sem, load_sem, basis_sem, own_send, plane_recv, fwd_plane, line_recv, fwd_send,
    meta_send, meta_recv, row_send, row_recv, col_send, col_recv, part_send, part_recv,
):
    planes = n // lines
    half = planes // 2
    direct = False
    docs = blk.shape[1]
    size = docs // CHUNKS
    clusters = owner_hbm.shape[0]
    share = counts_hbm.shape[0]
    order_bits = (n * docs - 1).bit_length()
    group_of = lambda keys: lax.shift_right_logical(keys, order_bits)
    me = lax.axis_index("row")
    z = me // lines
    line = me % lines

    def from_below(s, at):
        return (s >= 0) & (s < half) & (s < at) & (at <= planes - 2)

    def from_above(s, at):
        return (s < planes) & (at < s) & (at >= 0) & ((s == planes - 1) | ((s >= half) & (at >= half)))

    def piece(d, c):
        return blk.at[d, pl.ds(c * size, size)]

    def remote(src, dst, send, recv, device):
        return pltpu.make_async_remote_copy(
            src_ref=src, dst_ref=dst, send_sem=send, recv_sem=recv,
            device_id={"row": device}, device_id_type=MESH,
        )

    def block_copy(d, c, send, recv, device):
        return remote(piece(d, c), piece(d, c), send, recv, device)

    smalls = [
        pltpu.make_async_copy(source, target, small_sem.at[i])
        for i, (source, target) in enumerate(
            ((ids_hbm, ids), (order_hbm, order), (owner_hbm, owner), (counts_hbm, counts_here))
        )
    ]
    for copy in smalls:
        copy.start()
    basis_copy = pltpu.make_async_copy(basis_hbm, basis, basis_sem)
    basis_copy.start()
    loads = []
    for c in range(CHUNKS):
        part_rows = pl.ds(c * size, size)
        load = pltpu.make_async_copy(emb_hbm.at[part_rows], emb.at[part_rows], load_sem.at[c])
        load.start()
        loads.append(load)

    mates = [(q, me ^ q) for q in range(1, lines)]
    mates += [(lines + k, lax.rem(z + k, planes) * lines + line) for k in range(1, planes)]
    barrier = pltpu.get_barrier_semaphore()
    everyone = [(k, lax.rem(me + k, n)) for k in range(n - 1, 0, -1)]
    for _, d in everyone:
        pl.semaphore_signal(barrier, inc=1, device_id={"row": d}, device_id_type=MESH)

    def meta_copy(i, d):
        return remote(meta.at[me], meta.at[me], meta_send.at[i], meta_recv.at[me], d)

    for copy in smalls:
        copy.wait()
    own_ids = ids[...].reshape(1, docs)
    own_order = order[...].reshape(1, docs)
    meta[me] = lax.shift_left(own_ids, order_bits) + own_order

    goes_up = from_below(z, z + 1)
    goes_down = from_above(z, z - 1)

    def own_copies(c):
        copies = [(None, block_copy(me, c, own_send.at[0, c], plane_recv.at[line, c], me ^ 1))]
        if lines == 4:
            copies.append((None, block_copy(me, c, own_send.at[1, c], plane_recv.at[line, c], me ^ 2)))
        if planes > 1:
            up = jnp.minimum(me + lines, n - 1)
            down = jnp.maximum(me - lines, 0)
            copies.append((goes_up, block_copy(me, c, own_send.at[2, c], line_recv.at[z, c], up)))
            copies.append((goes_down, block_copy(me, c, own_send.at[3, c], line_recv.at[z, c], down)))
        if direct:
            copies = copies[::-1]
            up = jnp.minimum(me + 2 * lines, n - 1)
            down = jnp.maximum(me - 2 * lines, 0)
            copies.append((from_below(z, z + 2), block_copy(me, c, own_send.at[4, c], line_recv.at[z, c], up)))
            copies.append((z == planes - 1, block_copy(me, c, own_send.at[5, c], line_recv.at[z, c], down)))
        return copies

    def each(copies, act):
        for condition, copy in copies:
            if condition is None:
                act(copy)
            else:
                pl.when(condition)(functools.partial(act, copy))

    pl.semaphore_wait(barrier, n - 1)
    for i, d in mates:
        meta_copy(i, d).start()

    basis_copy.wait()
    for c in range(CHUNKS):
        loads[c].wait()
        projected = jnp.dot(
            emb[pl.ds(c * size, size), :], basis[...], preferred_element_type=jnp.float32
        )
        scale = lax.rsqrt(jnp.sum(projected * projected, axis=1, keepdims=True) + epsilon)
        blk[me, pl.ds(c * size, size), :] = (projected * scale).astype(jnp.bfloat16)
        each(own_copies(c)[::-1], lambda copy: copy.start())

    acc[...] = jnp.full_like(acc, -1.0)
    lane = lax.broadcasted_iota(jnp.int32, (1, clusters), 1) - me * share
    placed = jnp.zeros((1, clusters), jnp.int32)
    for k in range(share):
        placed = jnp.where(lane == k, counts_here[k], placed)
    part[me, :, clusters:] = placed.astype(jnp.float32)

    owned = (owner[...].reshape(1, clusters) == me).astype(jnp.float32)
    before = (
        lax.broadcasted_iota(jnp.int32, (clusters, clusters), 0)
        < lax.broadcasted_iota(jnp.int32, (clusters, clusters), 1)
    ).astype(jnp.bfloat16)
    per_owner = clusters // n
    many = jnp.broadcast_to(owned, (per_owner, clusters))
    rank = jnp.dot(many.astype(jnp.bfloat16), before, preferred_element_type=jnp.float32)
    wanted = lax.broadcasted_iota(jnp.int32, (per_owner, clusters), 0).astype(jnp.float32)
    pick = (many > 0.5) & (rank == wanted)

    for i, d in mates:
        remote(meta.at[d], meta.at[d], meta_send.at[i], meta_recv.at[d], d).wait_recv()

    for p in range(lines):
        keys = meta[z * lines + p]
        for i in range(0, docs, 128):
            column = jnp.transpose(jnp.broadcast_to(keys[:, i : i + 128], (128, 128)))
            kcol[pl.ds(p * docs + i, 128), :] = column
            ccol[pl.ds(p * docs + i, 128), :] = group_of(column)

    def plane_wait(p, c):
        block_copy(z * lines + p, c, own_send.at[0, c], plane_recv.at[p, c], me ^ 1).wait_recv()

    def line_wait(s, c):
        block_copy(s * lines + line, c, own_send.at[0, c], line_recv.at[s, c], me ^ 1).wait_recv()

    def forward(s, c, device):
        return block_copy(s * lines + line, c, fwd_send.at[s, c], line_recv.at[s, c], device)

    def arrivals(k):
        low, high = z - k, z + k
        below = from_below(low, z)
        above = from_above(high, z)
        if direct:
            return (
                (jnp.maximum(low, 0), below, below & (z < 0), jnp.minimum(me + lines, n - 1)),
                (
                    jnp.minimum(high, planes - 1),
                    above,
                    above & (z == planes - 2),
                    jnp.maximum(me - 2 * lines, 0),
                ),
            )
        return (
            (jnp.maximum(low, 0), below, below & from_below(low, z + 1), jnp.minimum(me + lines, n - 1)),
            (jnp.minimum(high, planes - 1), above, above & from_above(high, z - 1), jnp.maximum(me - lines, 0)),
        )

    def forward_step(k, c):
        for s, _, on, device in arrivals(k):
            @pl.when(on)
            def _():
                line_wait(s, c)
                forward(s, c, device).start()

    def diagonal_copy(c):
        return block_copy(me ^ 2, c, fwd_plane.at[c], plane_recv.at[line ^ 2, c], me ^ 1)

    for c in range(CHUNKS):
        forward_step(1, c)
        if lines == 4:
            plane_wait(line ^ 2, c)
            diagonal_copy(c).start()
    for c in range(CHUNKS):
        plane_wait(line ^ 1, c)
        if lines == 4:
            plane_wait(line ^ 3, c)

    def process(d, s, c, visitor):
        keys = blk[d, pl.ds(c * size, size), :]
        at = pl.ds(pl.multiple_of(c * size, size), size)
        lane_keys = meta[d, :, at]
        lane_groups = group_of(lane_keys)

        def one(p, carry):
            scores = lax.dot_general(
                blk[z * lines + p], keys, (((1,), (1,)), ((), ())), preferred_element_type=jnp.float32
            )
            rows = pl.ds(pl.multiple_of(p * docs, docs), docs)
            k_col, c_col = kcol[rows, :], ccol[rows, :]
            row_part = acc[rows, :] if visitor else None
            outs = []
            for i in range(0, size, 128):
                lk, lg = lane_keys[:, i : i + 128], lane_groups[:, i : i + 128]
                s_same = jnp.where(c_col == lg, scores[:, i : i + 128], -1.0)
                if visitor:
                    earlier = lk < k_col
                    row_part = jnp.maximum(row_part, jnp.where(earlier, s_same, -1.0))
                    for_lane = jnp.where(earlier, -1.0, s_same)
                else:
                    for_lane = jnp.where(k_col < lk, s_same, -1.0)
                outs.append(jnp.max(for_lane, axis=0, keepdims=True))
            if visitor:
                acc[rows, :] = row_part
            return jnp.maximum(carry, jnp.concatenate(outs, axis=1))

        result = lax.fori_loop(0, lines, one, jnp.full((1, size), -1.0, jnp.float32), unroll=True)
        if visitor:
            col[s, :, at] = result
        else:
            home[:, at] = result

    def col_copy(s, at, device):
        return remote(col.at[s], rc.at[at], col_send.at[s], col_recv.at[at], device)

    def process_step(k):
        for s, here, on, _ in arrivals(k):
            @pl.when(here)
            def _():
                @pl.loop(0, CHUNKS)
                def _(c):
                    @pl.when(jnp.logical_not(on))
                    def _():
                        line_wait(s, c)
                    process(s * lines + line, s, c, True)
                col_copy(s, z, s * lines + line).start()

    if planes > 2:
        forward_step(2, 0)

    @pl.loop(0, CHUNKS)
    def _(c):
        process(me, z, c, False)

    if planes > 2:
        for c in range(1, CHUNKS):
            forward_step(2, c)
    if planes > 1:
        process_step(1)

        @pl.loop(2, planes)
        def _(k):
            for c in range(CHUNKS):
                forward_step(k + 1, c)
            process_step(k)

    def row_copy(q):
        return remote(row.at[line ^ q], rr.at[line], row_send.at[q], row_recv.at[line], me ^ q)

    for q in [*range(lines - 1, 0, -1), 0]:
        rows = pl.ds(pl.multiple_of((line ^ q) * docs, docs), docs)
        row[line ^ q] = row_of(acc[rows, :], jnp.max)
        if q:
            row_copy(q).start()
    home[...] = jnp.maximum(home[...], row[line])
    for q in range(1, lines):
        remote(row.at[line], rr.at[line ^ q], row_send.at[q], row_recv.at[line ^ q], me ^ q).wait_recv()
        home[...] = jnp.maximum(home[...], rr[line ^ q])

    @pl.loop(0, planes)
    def _(at):
        @pl.when(from_below(z, at) | from_above(z, at))
        def _():
            remote(col.at[z], rc.at[at], col_send.at[z], col_recv.at[at], me ^ 1).wait_recv()
            home[...] = jnp.maximum(home[...], rc[at])

    best = home[...]
    best_ref[...] = best

    adds = jnp.where(own_order >= 1, best, 0.0)
    for i in range(0, clusters, 128):
        ids_row = lax.broadcasted_iota(jnp.int32, (128, 128), 0) + i
        total = jnp.zeros((128, 128), jnp.float32)
        for j in range(0, docs, 128):
            total += jnp.where(ids_row == own_ids[:, j : j + 128], adds[:, j : j + 128], 0.0)
        part[me, :, i : i + 128] = row_of(total, jnp.sum)

    def part_copy(k, d):
        return remote(part.at[me], part.at[me], part_send.at[k], part_recv.at[me], d)

    for k, d in everyone:
        part_copy(k, d).start()
    for k, d in everyone:
        remote(part.at[d], part.at[d], part_send.at[k], part_recv.at[d], d).wait_recv()
    totals = sum(part[d] for d in range(n))
    mean = totals[:, :clusters] / totals[:, clusters:]
    picked = jnp.where(pick, mean, 0.0)
    folded = sum(picked[:, i : i + 128] for i in range(0, clusters, 128))
    rest = jnp.zeros((128 - per_owner, 128), jnp.float32)
    scores_ref[...] = row_of(jnp.concatenate([folded, rest], axis=0), jnp.sum)[:, :per_owner]

    for c in range(CHUNKS):
        each(own_copies(c), lambda copy: copy.wait_send())
        if lines == 4:
            diagonal_copy(c).wait_send()

    for i, d in mates:
        meta_copy(i, d).wait_send()
    for k, d in everyone:
        part_copy(k, d).wait_send()

    for q in range(1, lines):
        row_copy(q).wait_send()

    @pl.loop(1, planes)
    def _(k):
        for s, here, on, device in arrivals(k):
            @pl.when(here)
            def _():
                col_copy(s, z, s * lines + line).wait_send()

            @pl.when(on)
            def _():
                for c in range(CHUNKS):
                    forward(s, c, device).wait_send()


def body(embeddings, basis, cluster_ids, member_order, owner_map, counts):
    n = lax.axis_size("row")
    docs, width = embeddings.shape
    kept = basis.shape[1]
    clusters = owner_map.shape[0]
    lines = 4 if n <= 16 else 2
    planes = n // lines
    share = counts.shape[0]
    vmem = functools.partial(pl.BlockSpec, memory_space=pltpu.VMEM)
    hbm = functools.partial(pl.BlockSpec, memory_space=pl.ANY)
    dma = pltpu.SemaphoreType.DMA
    f32, i32, bf16 = jnp.float32, jnp.int32, jnp.bfloat16
    best, scores = pl.pallas_call(
        functools.partial(kernel, n, lines),
        out_shape=(
            jax.ShapeDtypeStruct((1, docs), f32),
            jax.ShapeDtypeStruct((1, clusters // n), f32),
        ),
        in_specs=[hbm()] * 6,
        out_specs=(vmem(), vmem()),
        scratch_shapes=[
            pltpu.VMEM((docs,), i32),
            pltpu.VMEM((docs,), i32),
            pltpu.VMEM((clusters,), i32),
            pltpu.SMEM((share,), i32),
            pltpu.VMEM((docs, width), bf16),
            pltpu.VMEM((width, kept), bf16),
            pltpu.VMEM((n, docs, kept), bf16),
            pltpu.VMEM((n, 1, docs), i32),
            pltpu.VMEM((lines * docs, 128), i32),
            pltpu.VMEM((lines * docs, 128), i32),
            pltpu.VMEM((lines * docs, 128), f32),
            pltpu.VMEM((planes, 1, docs), f32),
            pltpu.VMEM((lines, 1, docs), f32),
            pltpu.VMEM((1, docs), f32),
            pltpu.VMEM((lines, 1, docs), f32),
            pltpu.VMEM((planes, 1, docs), f32),
            pltpu.VMEM((n, 1, 2 * clusters), f32),
            dma((4,)),
            dma((CHUNKS,)),
            dma,
            dma((6, CHUNKS)),
            dma((lines, CHUNKS)),
            dma((CHUNKS,)),
            dma((planes, CHUNKS)),
            dma((planes, CHUNKS)),
            dma((lines + planes,)),
            dma((n,)),
            dma((lines,)),
            dma((lines,)),
            dma((planes,)),
            dma((planes,)),
            dma((n,)),
            dma((n,)),
        ],
        compiler_params=pltpu.CompilerParams(
            collective_id=0, has_side_effects=True, vmem_limit_bytes=62 * 1024 * 1024 + 512 * 1024
        ),
        name="cluster_scores",
    )(embeddings, basis, cluster_ids, member_order, owner_map, counts)
    return best.reshape(-1), scores.reshape(-1)


def solution(mesh):
    in_specs = (
        P(("groups", "row"), None),
        P(),
        P(("groups", "row")),
        P(("groups", "row")),
        P("groups"),
        P(("groups", "row")),
    )
    out_specs = (P(("groups", "row")), P(("groups", "row")))
    return jax.shard_map(body, mesh=mesh, in_specs=in_specs, out_specs=out_specs, check_vma=False)
```

```python
import functools

import jax
import jax.numpy as jnp
from jax import lax
from jax.experimental import pallas as pl
from jax.experimental.pallas import tpu as pltpu
from jax.sharding import PartitionSpec as P

epsilon = 1e-06
MESH = pl.DeviceIdType.MESH
CHUNKS = 2


def row_of(tile, reduce):
    pieces = [
        reduce(jnp.transpose(tile[i : i + 128, :]), axis=0, keepdims=True)
        for i in range(0, tile.shape[0], 128)
    ]
    return pieces[0] if len(pieces) == 1 else jnp.concatenate(pieces, axis=1)


def kernel(
    n, lines, emb_hbm, basis_hbm, ids_hbm, order_hbm, owner_hbm, counts_hbm,
    best_ref, scores_ref,
    ids, order, owner, counts_here, emb, basis, blk, meta, kcol, ccol, acc, col, row, home, rr, rc, part,
    small_sem, load_sem, basis_sem, own_send, plane_recv, fwd_plane, line_recv, fwd_send,
    meta_send, meta_recv, row_send, row_recv, col_send, col_recv, part_send, part_recv,
):
    planes = n // lines
    half = planes // 2
    direct = False
    docs = blk.shape[1]
    size = docs // CHUNKS
    clusters = owner_hbm.shape[0]
    share = counts_hbm.shape[0]
    order_bits = (n * docs - 1).bit_length()
    group_of = lambda keys: lax.shift_right_logical(keys, order_bits)
    me = lax.axis_index("row")
    z = me // lines
    line = me % lines

    def from_below(s, at):
        return (s >= 0) & (s < half) & (s < at) & (at <= planes - 2)

    def from_above(s, at):
        return (s < planes) & (at < s) & (at >= 0) & ((s == planes - 1) | ((s >= half) & (at >= half)))

    def piece(d, c):
        return blk.at[d, pl.ds(c * size, size)]

    def remote(src, dst, send, recv, device):
        return pltpu.make_async_remote_copy(
            src_ref=src, dst_ref=dst, send_sem=send, recv_sem=recv,
            device_id={"row": device}, device_id_type=MESH,
        )

    def block_copy(d, c, send, recv, device):
        return remote(piece(d, c), piece(d, c), send, recv, device)

    smalls = [
        pltpu.make_async_copy(source, target, small_sem.at[i])
        for i, (source, target) in enumerate(
            ((ids_hbm, ids), (order_hbm, order), (owner_hbm, owner), (counts_hbm, counts_here))
        )
    ]
    for copy in smalls:
        copy.start()
    basis_copy = pltpu.make_async_copy(basis_hbm, basis, basis_sem)
    basis_copy.start()
    loads = []
    for c in range(CHUNKS):
        part_rows = pl.ds(c * size, size)
        load = pltpu.make_async_copy(emb_hbm.at[part_rows], emb.at[part_rows], load_sem.at[c])
        load.start()
        loads.append(load)

    mates = [(q, me ^ q) for q in range(1, lines)]
    mates += [(lines + k, lax.rem(z + k, planes) * lines + line) for k in range(1, planes)]
    barrier = pltpu.get_barrier_semaphore()
    everyone = [(k, lax.rem(me + k, n)) for k in range(n - 1, 0, -1)]
    for _, d in everyone:
        pl.semaphore_signal(barrier, inc=1, device_id={"row": d}, device_id_type=MESH)

    def meta_copy(i, d):
        return remote(meta.at[me], meta.at[me], meta_send.at[i], meta_recv.at[me], d)

    for copy in smalls:
        copy.wait()
    own_ids = ids[...].reshape(1, docs)
    own_order = order[...].reshape(1, docs)
    meta[me] = lax.shift_left(own_ids, order_bits) + own_order

    goes_up = from_below(z, z + 1)
    goes_down = from_above(z, z - 1)

    def own_copies(c):
        copies = [(None, block_copy(me, c, own_send.at[0, c], plane_recv.at[line, c], me ^ 1))]
        if lines == 4:
            copies.append((None, block_copy(me, c, own_send.at[1, c], plane_recv.at[line, c], me ^ 2)))
        if planes > 1:
            up = jnp.minimum(me + lines, n - 1)
            down = jnp.maximum(me - lines, 0)
            copies.append((goes_up, block_copy(me, c, own_send.at[2, c], line_recv.at[z, c], up)))
            copies.append((goes_down, block_copy(me, c, own_send.at[3, c], line_recv.at[z, c], down)))
        if direct:
            copies = copies[::-1]
            up = jnp.minimum(me + 2 * lines, n - 1)
            down = jnp.maximum(me - 2 * lines, 0)
            copies.append((from_below(z, z + 2), block_copy(me, c, own_send.at[4, c], line_recv.at[z, c], up)))
            copies.append((z == planes - 1, block_copy(me, c, own_send.at[5, c], line_recv.at[z, c], down)))
        return copies

    def each(copies, act):
        for condition, copy in copies:
            if condition is None:
                act(copy)
            else:
                pl.when(condition)(functools.partial(act, copy))

    acc[...] = jnp.full_like(acc, -1.0)
    lane = lax.broadcasted_iota(jnp.int32, (1, clusters), 1) - me * share
    placed = jnp.zeros((1, clusters), jnp.int32)
    for k in range(share):
        placed = jnp.where(lane == k, counts_here[k], placed)
    part[me, :, clusters:] = placed.astype(jnp.float32)

    owned = (owner[...].reshape(1, clusters) == me).astype(jnp.float32)
    before = (
        lax.broadcasted_iota(jnp.int32, (clusters, clusters), 0)
        < lax.broadcasted_iota(jnp.int32, (clusters, clusters), 1)
    ).astype(jnp.bfloat16)
    per_owner = clusters // n
    many = jnp.broadcast_to(owned, (per_owner, clusters))
    rank = jnp.dot(many.astype(jnp.bfloat16), before, preferred_element_type=jnp.float32)
    wanted = lax.broadcasted_iota(jnp.int32, (per_owner, clusters), 0).astype(jnp.float32)
    pick = (many > 0.5) & (rank == wanted)

    pl.semaphore_wait(barrier, n - 1)
    for i, d in mates:
        meta_copy(i, d).start()

    basis_copy.wait()
    for c in range(CHUNKS):
        loads[c].wait()
        projected = jnp.dot(
            emb[pl.ds(c * size, size), :], basis[...], preferred_element_type=jnp.float32
        )
        scale = lax.rsqrt(jnp.sum(projected * projected, axis=1, keepdims=True) + epsilon)
        blk[me, pl.ds(c * size, size), :] = (projected * scale).astype(jnp.bfloat16)
        each(own_copies(c)[::-1], lambda copy: copy.start())


    for i, d in mates:
        remote(meta.at[d], meta.at[d], meta_send.at[i], meta_recv.at[d], d).wait_recv()

    for p in range(lines):
        keys = meta[z * lines + p]
        for i in range(0, docs, 128):
            column = jnp.transpose(jnp.broadcast_to(keys[:, i : i + 128], (128, 128)))
            kcol[pl.ds(p * docs + i, 128), :] = column
            ccol[pl.ds(p * docs + i, 128), :] = group_of(column)

    def plane_wait(p, c):
        block_copy(z * lines + p, c, own_send.at[0, c], plane_recv.at[p, c], me ^ 1).wait_recv()

    def line_wait(s, c):
        block_copy(s * lines + line, c, own_send.at[0, c], line_recv.at[s, c], me ^ 1).wait_recv()

    def forward(s, c, device):
        return block_copy(s * lines + line, c, fwd_send.at[s, c], line_recv.at[s, c], device)

    def arrivals(k):
        low, high = z - k, z + k
        below = from_below(low, z)
        above = from_above(high, z)
        if direct:
            return (
                (jnp.maximum(low, 0), below, below & (z < 0), jnp.minimum(me + lines, n - 1)),
                (
                    jnp.minimum(high, planes - 1),
                    above,
                    above & (z == planes - 2),
                    jnp.maximum(me - 2 * lines, 0),
                ),
            )
        return (
            (jnp.maximum(low, 0), below, below & from_below(low, z + 1), jnp.minimum(me + lines, n - 1)),
            (jnp.minimum(high, planes - 1), above, above & from_above(high, z - 1), jnp.maximum(me - lines, 0)),
        )

    def forward_step(k, c):
        for s, _, on, device in arrivals(k):
            @pl.when(on)
            def _():
                line_wait(s, c)
                forward(s, c, device).start()

    def diagonal_copy(c):
        return block_copy(me ^ 2, c, fwd_plane.at[c], plane_recv.at[line ^ 2, c], me ^ 1)

    for c in range(CHUNKS):
        forward_step(1, c)
        if lines == 4:
            plane_wait(line ^ 2, c)
            diagonal_copy(c).start()
    for c in range(CHUNKS):
        plane_wait(line ^ 1, c)
        if lines == 4:
            plane_wait(line ^ 3, c)

    def process(d, s, c, visitor):
        keys = blk[d, pl.ds(c * size, size), :]
        at = pl.ds(pl.multiple_of(c * size, size), size)
        lane_keys = meta[d, :, at]
        lane_groups = group_of(lane_keys)

        def one(p, carry):
            scores = lax.dot_general(
                blk[z * lines + p], keys, (((1,), (1,)), ((), ())), preferred_element_type=jnp.float32
            )
            rows = pl.ds(pl.multiple_of(p * docs, docs), docs)
            k_col, c_col = kcol[rows, :], ccol[rows, :]
            row_part = acc[rows, :] if visitor else None
            outs = []
            for i in range(0, size, 128):
                lk, lg = lane_keys[:, i : i + 128], lane_groups[:, i : i + 128]
                s_same = jnp.where(c_col == lg, scores[:, i : i + 128], -1.0)
                if visitor:
                    earlier = lk < k_col
                    row_part = jnp.maximum(row_part, jnp.where(earlier, s_same, -1.0))
                    for_lane = jnp.where(earlier, -1.0, s_same)
                else:
                    for_lane = jnp.where(k_col < lk, s_same, -1.0)
                outs.append(jnp.max(for_lane, axis=0, keepdims=True))
            if visitor:
                acc[rows, :] = row_part
            return jnp.maximum(carry, jnp.concatenate(outs, axis=1))

        result = lax.fori_loop(0, lines, one, jnp.full((1, size), -1.0, jnp.float32), unroll=True)
        if visitor:
            col[s, :, at] = result
        else:
            home[:, at] = result

    def col_copy(s, at, device):
        return remote(col.at[s], rc.at[at], col_send.at[s], col_recv.at[at], device)

    def process_step(k):
        for s, here, on, _ in arrivals(k):
            @pl.when(here)
            def _():
                @pl.loop(0, CHUNKS)
                def _(c):
                    @pl.when(jnp.logical_not(on))
                    def _():
                        line_wait(s, c)
                    process(s * lines + line, s, c, True)
                col_copy(s, z, s * lines + line).start()

    if planes > 2:
        forward_step(2, 0)

    @pl.loop(0, CHUNKS)
    def _(c):
        process(me, z, c, False)

    if planes > 2:
        for c in range(1, CHUNKS):
            forward_step(2, c)
    if planes > 1:
        process_step(1)

        @pl.loop(2, planes)
        def _(k):
            for c in range(CHUNKS):
                forward_step(k + 1, c)
            process_step(k)

    def row_copy(q):
        return remote(row.at[line ^ q], rr.at[line], row_send.at[q], row_recv.at[line], me ^ q)

    for q in [*range(lines - 1, 0, -1), 0]:
        rows = pl.ds(pl.multiple_of((line ^ q) * docs, docs), docs)
        row[line ^ q] = row_of(acc[rows, :], jnp.max)
        if q:
            row_copy(q).start()
    home[...] = jnp.maximum(home[...], row[line])
    for q in range(1, lines):
        remote(row.at[line], rr.at[line ^ q], row_send.at[q], row_recv.at[line ^ q], me ^ q).wait_recv()
        home[...] = jnp.maximum(home[...], rr[line ^ q])

    @pl.loop(0, planes)
    def _(at):
        @pl.when(from_below(z, at) | from_above(z, at))
        def _():
            remote(col.at[z], rc.at[at], col_send.at[z], col_recv.at[at], me ^ 1).wait_recv()
            home[...] = jnp.maximum(home[...], rc[at])

    best = home[...]
    best_ref[...] = best

    adds = jnp.where(own_order >= 1, best, 0.0)
    for i in range(0, clusters, 128):
        ids_row = lax.broadcasted_iota(jnp.int32, (128, 128), 0) + i
        total = jnp.zeros((128, 128), jnp.float32)
        for j in range(0, docs, 128):
            total += jnp.where(ids_row == own_ids[:, j : j + 128], adds[:, j : j + 128], 0.0)
        part[me, :, i : i + 128] = row_of(total, jnp.sum)

    def part_copy(k, d):
        return remote(part.at[me], part.at[me], part_send.at[k], part_recv.at[me], d)

    for k, d in everyone:
        part_copy(k, d).start()
    for k, d in everyone:
        remote(part.at[d], part.at[d], part_send.at[k], part_recv.at[d], d).wait_recv()
    totals = sum(part[d] for d in range(n))
    mean = totals[:, :clusters] / totals[:, clusters:]
    picked = jnp.where(pick, mean, 0.0)
    folded = sum(picked[:, i : i + 128] for i in range(0, clusters, 128))
    rest = jnp.zeros((128 - per_owner, 128), jnp.float32)
    scores_ref[...] = row_of(jnp.concatenate([folded, rest], axis=0), jnp.sum)[:, :per_owner]

    for c in range(CHUNKS):
        each(own_copies(c), lambda copy: copy.wait_send())
        if lines == 4:
            diagonal_copy(c).wait_send()

    for i, d in mates:
        meta_copy(i, d).wait_send()
    for k, d in everyone:
        part_copy(k, d).wait_send()

    for q in range(1, lines):
        row_copy(q).wait_send()

    @pl.loop(1, planes)
    def _(k):
        for s, here, on, device in arrivals(k):
            @pl.when(here)
            def _():
                col_copy(s, z, s * lines + line).wait_send()

            @pl.when(on)
            def _():
                for c in range(CHUNKS):
                    forward(s, c, device).wait_send()


def body(embeddings, basis, cluster_ids, member_order, owner_map, counts):
    n = lax.axis_size("row")
    docs, width = embeddings.shape
    kept = basis.shape[1]
    clusters = owner_map.shape[0]
    lines = 4 if n <= 16 else 2
    planes = n // lines
    share = counts.shape[0]
    vmem = functools.partial(pl.BlockSpec, memory_space=pltpu.VMEM)
    hbm = functools.partial(pl.BlockSpec, memory_space=pl.ANY)
    dma = pltpu.SemaphoreType.DMA
    f32, i32, bf16 = jnp.float32, jnp.int32, jnp.bfloat16
    best, scores = pl.pallas_call(
        functools.partial(kernel, n, lines),
        out_shape=(
            jax.ShapeDtypeStruct((1, docs), f32),
            jax.ShapeDtypeStruct((1, clusters // n), f32),
        ),
        in_specs=[hbm()] * 6,
        out_specs=(vmem(), vmem()),
        scratch_shapes=[
            pltpu.VMEM((docs,), i32),
            pltpu.VMEM((docs,), i32),
            pltpu.VMEM((clusters,), i32),
            pltpu.SMEM((share,), i32),
            pltpu.VMEM((docs, width), bf16),
            pltpu.VMEM((width, kept), bf16),
            pltpu.VMEM((n, docs, kept), bf16),
            pltpu.VMEM((n, 1, docs), i32),
            pltpu.VMEM((lines * docs, 128), i32),
            pltpu.VMEM((lines * docs, 128), i32),
            pltpu.VMEM((lines * docs, 128), f32),
            pltpu.VMEM((planes, 1, docs), f32),
            pltpu.VMEM((lines, 1, docs), f32),
            pltpu.VMEM((1, docs), f32),
            pltpu.VMEM((lines, 1, docs), f32),
            pltpu.VMEM((planes, 1, docs), f32),
            pltpu.VMEM((n, 1, 2 * clusters), f32),
            dma((4,)),
            dma((CHUNKS,)),
            dma,
            dma((6, CHUNKS)),
            dma((lines, CHUNKS)),
            dma((CHUNKS,)),
            dma((planes, CHUNKS)),
            dma((planes, CHUNKS)),
            dma((lines + planes,)),
            dma((n,)),
            dma((lines,)),
            dma((lines,)),
            dma((planes,)),
            dma((planes,)),
            dma((n,)),
            dma((n,)),
        ],
        compiler_params=pltpu.CompilerParams(
            collective_id=0, has_side_effects=True, vmem_limit_bytes=62 * 1024 * 1024 + 512 * 1024
        ),
        name="cluster_scores",
    )(embeddings, basis, cluster_ids, member_order, owner_map, counts)
    return best.reshape(-1), scores.reshape(-1)


def solution(mesh):
    in_specs = (
        P(("groups", "row"), None),
        P(),
        P(("groups", "row")),
        P(("groups", "row")),
        P("groups"),
        P(("groups", "row")),
    )
    out_specs = (P(("groups", "row")), P(("groups", "row")))
    return jax.shard_map(body, mesh=mesh, in_specs=in_specs, out_specs=out_specs, check_vma=False)
```
